32 devices in a mesh: groups: 2 (over x), tensor: 4 (over y, core), dp: 4 (over z).
Axes of the slice: x: 2, y: 2, z: 4, core: 2. Of those that a mesh axis runs over, the one named last changes fastest.
Arguments:
- layer_inputs: bfloat16 [2, 16, 512, 28672], P(None, ('groups', 'dp'), None, 'tensor'), parts along dimension 1, may hold values from -6 to 6
- output_grads: bfloat16 [2, 16, 512, 8192], P(None, ('groups', 'dp'), None, 'tensor'), parts along dimension 1, may hold values from -6 to 6
- in_proj: bfloat16 [2, 28672, 32], P(None, 'tensor'), may hold values from -0.03125 to 0.03125
- out_proj: bfloat16 [2, 8192, 32], P(None, 'tensor'), may hold values from -0.0625 to 0.0625
- valid_counts: int32 [16], P(('groups', 'dp')), parts along dimension 0, may hold values from 128 to 512
- assignment: int32 [16], P('groups'), parts along dimension 0, may hold values from 0 to 7, each once
Outputs:
- seq_grads: float32 [16, 2048], P(('groups', 'dp'), 'tensor'), parts along dimension 0
- fisher: float32 [4096, 2048], P(('groups', 'dp'), 'tensor'), parts along dimension 0
The draws below stay inside these ranges and needn't reach their ends.
There are 2 independent parts, one for each index of `groups`. The reference program is written for one: setup_inputs(seed, part) draws one part's arguments, and reference() takes and returns one part's arrays. A program takes and returns all parts, laid end to end along the dimension named above; an argument that names none is the same for every part. Nothing has to cross between parts.
All inputs are finite; a program needn't handle non-finite values.
Results may differ from the reference program's by a relative error of at most 0.0003.
Values sent between devices are 32-bit elements; how exact they have to be, the bound alone decides.
No kernel may reach another device: no remote copies, remote signals or barrier semaphores. Data moves between devices by JAX's collectives and lax.ppermute only.
A program may use at most 128 MiB of HBM per device.

```python
import jax
import jax.numpy as jnp
from jax import lax

D = 8192
FF = 28672
RANK = 32
LAYERS = 2
SEQ_LEN = 512
SEQS = 8


def draw_valid_counts(key, part):
    key = jax.random.fold_in(key, 7)
    counts = jax.random.randint(key, (SEQS,), SEQ_LEN // 4, SEQ_LEN + 1).astype(jnp.int32)
    counts = counts.at[0].set(SEQ_LEN)
    counts = counts.at[1].set(SEQ_LEN // 4)
    return counts


def steps_of(own_key, shape, pieces, least, high):
    def one(dim, blocks):
        draws = jax.random.uniform(jax.random.fold_in(jax.random.fold_in(own_key, 6), dim), (blocks,), jnp.float32, least / len(pieces), high / len(pieces))
        return jnp.repeat(jnp.exp(draws), shape[dim] // blocks).reshape((-1,) + (1,) * (len(shape) - dim - 1))

    loudness = one(*pieces[0])
    for cut in pieces[1:]:
        loudness = loudness * one(*cut)
    return loudness


def normal_values(own_key, extent, deviation, most, split=(), kind=jnp.bfloat16):
    level = steps_of(own_key, extent, split, -0.22, 0.18) if split else 1.0
    result = jax.random.normal(own_key, extent, jnp.float32) * deviation * level
    return jnp.minimum(jnp.maximum(result, -most), most).astype(kind)


def setup_inputs(seed: int = 0, part: int = 0) -> dict:
    splits = jax.random.split(jax.random.key(seed), 7)
    own_keys = jax.random.split(jax.random.fold_in(splits[6], part), 7)
    return {
        "layer_inputs": normal_values(own_keys[0], (LAYERS, SEQS, SEQ_LEN, FF), 1.0, 6.0, ((1, 4), (3, 4))),
        "output_grads": normal_values(own_keys[1], (LAYERS, SEQS, SEQ_LEN, D), 1.0, 6.0, ((1, 4), (3, 4))),
        "in_proj": normal_values(splits[2], (LAYERS, FF, RANK), FF ** -0.5, 0.03125, ((1, 4),)),
        "out_proj": normal_values(splits[3], (LAYERS, D, RANK), D ** -0.5, 0.0625, ((1, 4),)),
        "valid_counts": draw_valid_counts(jax.random.fold_in(jax.random.fold_in(splits[6], part), 71), part),
        "assignment": jax.random.permutation(own_keys[5], SEQS).astype(jnp.int32),
    }


def reference(layer_inputs, output_grads, in_proj, out_proj, valid_counts, assignment):
    positions = jnp.arange(SEQ_LEN, dtype=jnp.int32)
    keep = (positions[None, :] < valid_counts[:, None]).astype(jnp.float32)
    blocks = []
    for layer in range(LAYERS):
        in_weight = in_proj[layer].astype(jnp.float32)
        out_weight = out_proj[layer].astype(jnp.float32)

        def one_sequence(operands):
            inputs_seq, grads_seq, keep_seq = operands
            inner = jnp.dot(inputs_seq.astype(jnp.float32), in_weight, precision=lax.Precision.HIGHEST) * keep_seq[:, None]
            outer = jnp.dot(grads_seq.astype(jnp.float32), out_weight, precision=lax.Precision.HIGHEST)
            product = jnp.dot(outer.T, inner, precision=lax.Precision.HIGHEST)
            return product.reshape(RANK * RANK)
        blocks.append(lax.map(one_sequence, (layer_inputs[layer], output_grads[layer], keep)))
    vectors = jnp.concatenate(blocks, axis=1) * (SEQ_LEN ** -0.5)
    seq_grads = jnp.zeros_like(vectors).at[assignment].set(vectors)
    fisher = jnp.dot(vectors.T, vectors, precision=lax.Precision.HIGHEST) / SEQS
    return seq_grads, fisher
```

```python
import functools

import jax
import jax.numpy as jnp
from jax import lax
from jax.experimental import pallas as pl
from jax.experimental.pallas import tpu as pltpu
from jax.sharding import PartitionSpec as P

NT = (((1,), (1,)), ((), ()))
TN = (((0,), (0,)), ((), ()))


def pieces(value):
    high = value.astype(jnp.bfloat16)
    low = (value - high.astype(jnp.float32)).astype(jnp.bfloat16)
    return high, low


def project_kernel(step, width_x, width_g, depth, counts, x, g, wi, wo, send, keep, xb, gb, wib, wob, sems, wsems):
    layers, rank = wi.shape[0], wi.shape[1]
    tokens = x.shape[2]
    blocks = tokens // step
    core = lax.rem(lax.axis_index("tensor"), 2)
    slots = (1 - core, core)
    valid = [counts[s] for s in slots]
    used = [jnp.clip((v + (step - 1)) // step, 1, blocks) for v in valid]
    jobs = []
    for j in range(2):
        for l in range(layers):
            for k in range(0, x.shape[3], width_x):
                jobs.append((0, j, l, k, width_x))
            for k in range(0, g.shape[3], width_g):
                jobs.append((1, j, l, k, width_g))

    def copy(i, v):
        which, j, l, k, width = jobs[i]
        src, dst = ((x, xb), (g, gb))[which]
        rows, cols = pl.ds(0, step * v), pl.ds(k, width)
        return pltpu.make_async_copy(src.at[l, slots[j], rows, cols], dst.at[l, j, rows, cols], sems.at[i])

    def start(i):
        if i < len(jobs):
            for v in range(1, blocks + 1):

                @pl.when(used[jobs[i][1]] == v)
                def _():
                    copy(i, v).start()

    weights = [pltpu.make_async_copy(wi, wib, wsems.at[0]), pltpu.make_async_copy(wo, wob, wsems.at[1])]
    for c in weights:
        c.start()
    for i in range(depth):
        start(i)
    send[...] = jnp.zeros_like(send)
    keep[...] = jnp.zeros_like(keep)
    for c in weights:
        c.wait()
    for i, (which, j, l, k, width) in enumerate(jobs):
        start(i + depth)
        data, weight = ((xb, wib), (gb, wob))[which]
        out = (send, keep)[j]
        first = (rank, 0)[which]
        last = k + width == data.shape[3]
        for v in range(1, blocks + 1):

            @pl.when(used[j] == v)
            def _():
                copy(i, v).wait()
                n = step * v
                d = lax.dot_general(
                    weight[l, :, k : k + width], data[l, j, 0:n, k : k + width], NT, preferred_element_type=jnp.float32
                )
                if k > 0:
                    d = d + out[l, first : first + rank, 0:n]
                if which == 0 and last:
                    d = jnp.where(lax.broadcasted_iota(jnp.int32, (rank, n), 1) < valid[j], d, 0.0)
                out[l, first : first + rank, 0:n] = d


def project(layer_inputs, output_grads, in_proj, out_proj, valid_counts):
    layers, seqs, tokens, ff = layer_inputs.shape
    d = output_grads.shape[3]
    rank = in_proj.shape[2]
    width_x, width_g = ff // 4, d
    jobs = 2 * layers * (ff // width_x + d // width_g)
    anywhere = pl.BlockSpec(memory_space=pl.ANY)
    out = jax.ShapeDtypeStruct((layers, 2 * rank, tokens), jnp.float32)
    return pl.pallas_call(
        functools.partial(project_kernel, tokens // 4, width_x, width_g, 3),
        out_shape=(out, out),
        in_specs=[pl.BlockSpec(memory_space=pltpu.SMEM)] + [anywhere] * 4,
        out_specs=(pl.BlockSpec(memory_space=pltpu.VMEM),) * 2,
        scratch_shapes=[
            pltpu.VMEM((layers, seqs, tokens, ff), jnp.bfloat16),
            pltpu.VMEM((layers, seqs, tokens, d), jnp.bfloat16),
            pltpu.VMEM((layers, rank, ff), jnp.bfloat16),
            pltpu.VMEM((layers, rank, d), jnp.bfloat16),
            pltpu.SemaphoreType.DMA((jobs,)),
            pltpu.SemaphoreType.DMA((2,)),
        ],
        compiler_params=pltpu.CompilerParams(vmem_limit_bytes=48 * 2**20),
        name="project",
    )(valid_counts, layer_inputs, output_grads, jnp.swapaxes(in_proj, 1, 2), jnp.swapaxes(out_proj, 1, 2))


def product_kernel(scale, own, received, out, square):
    layers, rank = own.shape[0], own.shape[1] // 2
    per_row = 128 // rank
    rows = rank // per_row
    for l in range(layers):
        outer_high, outer_low = pieces(own[l, 0:rank] + received[l, 0:rank])
        inner_high, inner_low = pieces(own[l, rank:] + received[l, rank:])
        both = lax.dot_general(
            jnp.concatenate([outer_high, outer_low], axis=0), inner_high, NT, preferred_element_type=jnp.float32
        )
        third = lax.dot_general(outer_high, inner_low, NT, preferred_element_type=jnp.float32)
        square[l] = (both[0:rank] + (both[rank:] + third)) * scale
        out[l * rows : (l + 1) * rows, :] = jnp.concatenate(
            [square[l, pl.ds(r, rows, stride=per_row), :] for r in range(per_row)], axis=1
        )


def product(own, received):
    layers, double, tokens = own.shape
    rank = double // 2
    return pl.pallas_call(
        functools.partial(product_kernel, tokens ** (-0.5)),
        out_shape=jax.ShapeDtypeStruct((layers * rank * rank // 128, 128), jnp.float32),
        in_specs=[pl.BlockSpec(memory_space=pltpu.VMEM)] * 2,
        out_specs=pl.BlockSpec(memory_space=pltpu.VMEM),
        scratch_shapes=[pltpu.VMEM((layers, rank, rank), jnp.float32)],
        name="product",
    )(own, received)


def gram_kernel(assignment, vectors, seq_grads, fisher):
    total = vectors.shape[0]
    local = seq_grads.shape[0]
    tensor, dp = lax.axis_index("tensor"), lax.axis_index("dp")
    core = lax.rem(tensor, 2)
    row_lanes, col_lanes = fisher.shape[0] // 128, fisher.shape[1] // 128
    rows = jnp.concatenate([vectors[:, dp * row_lanes + r, :] for r in range(row_lanes)], axis=1)
    cols = jnp.concatenate([vectors[:, tensor * col_lanes + r, :] for r in range(col_lanes)], axis=1)
    rows_high, rows_low = pieces(rows)
    cols_high, cols_low = pieces(cols)
    fisher[...] = lax.dot_general(
        jnp.concatenate([rows_high, rows_high, rows_low], axis=0),
        jnp.concatenate([cols_high, cols_low, cols_high], axis=0),
        TN,
        preferred_element_type=jnp.float32,
    ) * (1.0 / total)
    for r in range(local):
        chosen = jnp.zeros((1, cols.shape[1]), jnp.float32)
        for place in range(total):
            slot = lax.bitwise_xor(dp, place % (total // 2)) * 2 + lax.bitwise_xor(core, place // (total // 2))
            chosen = jnp.where(assignment[slot] == dp * local + r, cols[place : place + 1, :], chosen)
        seq_grads[r : r + 1, :] = chosen


def gram(vectors, assignment, local, row_width, col_width):
    return pl.pallas_call(
        gram_kernel,
        out_shape=(
            jax.ShapeDtypeStruct((local, col_width), jnp.float32),
            jax.ShapeDtypeStruct((row_width, col_width), jnp.float32),
        ),
        in_specs=[pl.BlockSpec(memory_space=pltpu.SMEM), pl.BlockSpec(memory_space=pltpu.VMEM)],
        out_specs=(pl.BlockSpec(memory_space=pltpu.VMEM),) * 2,
        name="gram",
    )(assignment, vectors)


def swap(value, axis, bit):
    size = lax.axis_size(axis)
    return lax.ppermute(value, axis, [(i, i ^ bit) for i in range(size)])


def two_level(layer_inputs, output_grads, in_proj, out_proj, valid_counts, assignment):
    layers, local = layer_inputs.shape[:2]
    rank = in_proj.shape[2]
    feat = layers * rank * rank
    send, keep = project(layer_inputs, output_grads, in_proj, out_proj, valid_counts)
    chip = keep + swap(send, "tensor", 1)
    vector = product(chip, swap(chip, "tensor", 2))
    gathered = vector[None]
    for bit in (1, 2):
        gathered = jnp.concatenate([gathered, swap(gathered, "dp", bit)], axis=0)
    gathered = jnp.concatenate([gathered, swap(gathered, "tensor", 1)], axis=0)
    return gram(gathered, assignment, local, feat // lax.axis_size("dp"), feat // lax.axis_size("tensor"))


def any_sizes(layer_inputs, output_grads, in_proj, out_proj, valid_counts, assignment):
    layers, local, tokens = layer_inputs.shape[:3]
    rank = in_proj.shape[2]
    position = jnp.arange(tokens, dtype=jnp.int32)
    keep = (position[None, :] < valid_counts[:, None]).astype(jnp.float32)
    outer = jnp.einsum("lstd,ldr->lsrt", output_grads, out_proj, preferred_element_type=jnp.float32)
    inner = jnp.einsum("lstf,lfr->lsrt", layer_inputs, in_proj, preferred_element_type=jnp.float32)
    summed = lax.psum(jnp.concatenate([outer, inner * keep[None, :, None, :]], axis=2), "tensor")
    product = jnp.einsum(
        "lsit,lsjt->slij", summed[:, :, :rank], summed[:, :, rank:], precision=lax.Precision.HIGHEST
    )
    vectors = product.reshape(local, layers * rank * rank) * tokens ** (-0.5)
    gathered = lax.all_gather(vectors, "dp", axis=0, tiled=True)
    total, feat = gathered.shape
    dp_index, tensor_index = lax.axis_index("dp"), lax.axis_index("tensor")
    row_width, col_width = feat // lax.axis_size("dp"), feat // lax.axis_size("tensor")
    cols = lax.dynamic_slice_in_dim(gathered, tensor_index * col_width, col_width, 1)
    rows = lax.dynamic_slice_in_dim(gathered, dp_index * row_width, row_width, 1)
    fisher = lax.dot_general(rows, cols, TN, precision=lax.Precision.HIGHEST) / total
    owners = dp_index * local + jnp.arange(local, dtype=jnp.int32)
    selector = (assignment[None, :] == owners[:, None]).astype(jnp.float32)
    return jnp.dot(selector, cols, precision=lax.Precision.HIGHEST), fisher


def on_device(*arrays):
    local = arrays[0].shape[1]
    if lax.axis_size("tensor") == 4 and lax.axis_size("dp") == 4 and local == 2:
        return two_level(*arrays)
    return any_sizes(*arrays)


def solution(mesh):
    return jax.shard_map(
        on_device,
        mesh=mesh,
        in_specs=(
            P(None, ("groups", "dp"), None, "tensor"),
            P(None, ("groups", "dp"), None, "tensor"),
            P(None, "tensor", None),
            P(None, "tensor", None),
            P(("groups", "dp")),
            P("groups"),
        ),
        out_specs=(P(("groups", "dp"), "tensor"), P(("groups", "dp"), "tensor")),
        check_vma=False,
    )
```

```python
import functools

import jax
import jax.numpy as jnp
from jax import lax
from jax.experimental import pallas as pl
from jax.experimental.pallas import tpu as pltpu
from jax.sharding import PartitionSpec as P

NT = (((1,), (1,)), ((), ()))
TN = (((0,), (0,)), ((), ()))


def pieces(value):
    high = value.astype(jnp.bfloat16)
    low = (value - high.astype(jnp.float32)).astype(jnp.bfloat16)
    return high, low


def project_kernel(step, width_x, width_g, depth, counts, x, g, wi, wo, send, keep, xb, gb, wib, wob, sems, wsems):
    layers, rank = wi.shape[0], wi.shape[1]
    tokens = x.shape[2]
    blocks = tokens // step
    core = lax.rem(lax.axis_index("tensor"), 2)
    slots = (1 - core, core)
    valid = [counts[s] for s in slots]
    used = [jnp.clip((v + (step - 1)) // step, 1, blocks) for v in valid]
    jobs = []
    for j in range(2):
        for l in range(layers):
            for k in range(0, x.shape[3], width_x):
                jobs.append((0, j, l, k, width_x))
            for k in range(0, g.shape[3], width_g):
                jobs.append((1, j, l, k, width_g))

    def copy(i, v):
        which, j, l, k, width = jobs[i]
        src, dst = ((x, xb), (g, gb))[which]
        rows, cols = pl.ds(0, step * v), pl.ds(k, width)
        return pltpu.make_async_copy(src.at[l, slots[j], rows, cols], dst.at[l, j, rows, cols], sems.at[i])

    def start(i):
        if i < len(jobs):
            for v in range(1, blocks + 1):

                @pl.when(used[jobs[i][1]] == v)
                def _():
                    copy(i, v).start()

    weights = [pltpu.make_async_copy(wi, wib, wsems.at[0]), pltpu.make_async_copy(wo, wob, wsems.at[1])]
    for c in weights:
        c.start()
    for i in range(depth):
        start(i)
    send[...] = jnp.zeros_like(send)
    keep[...] = jnp.zeros_like(keep)
    for c in weights:
        c.wait()
    for i, (which, j, l, k, width) in enumerate(jobs):
        start(i + depth)
        data, weight = ((xb, wib), (gb, wob))[which]
        out = (send, keep)[j]
        first = (rank, 0)[which]
        last = k + width == data.shape[3]
        for v in range(1, blocks + 1):

            @pl.when(used[j] == v)
            def _():
                copy(i, v).wait()
                n = step * v
                d = lax.dot_general(
                    weight[l, :, k : k + width], data[l, j, 0:n, k : k + width], NT, preferred_element_type=jnp.float32
                )
                if k > 0:
                    d = d + out[l, first : first + rank, 0:n]
                if which == 0 and last:
                    d = jnp.where(lax.broadcasted_iota(jnp.int32, (rank, n), 1) < valid[j], d, 0.0)
                out[l, first : first + rank, 0:n] = d


def project(layer_inputs, output_grads, in_proj, out_proj, valid_counts):
    layers, seqs, tokens, ff = layer_inputs.shape
    d = output_grads.shape[3]
    rank = in_proj.shape[2]
    width_x, width_g = ff // 4, d
    jobs = 2 * layers * (ff // width_x + d // width_g)
    anywhere = pl.BlockSpec(memory_space=pl.ANY)
    out = pltpu.VMEM((layers, 2 * rank, tokens), jnp.float32)
    operands = (valid_counts, layer_inputs, output_grads, jnp.swapaxes(in_proj, 1, 2), jnp.swapaxes(out_proj, 1, 2))
    return pl.pallas_call(
        functools.partial(project_kernel, tokens // 4, width_x, width_g, 3),
        out_shape=(out, out),
        in_specs=[pl.BlockSpec(memory_space=pltpu.SMEM)] + [anywhere] * 4,
        out_specs=(pl.BlockSpec(memory_space=pltpu.VMEM),) * 2,
        scratch_shapes=[
            pltpu.VMEM((layers, seqs, tokens, ff), jnp.bfloat16),
            pltpu.VMEM((layers, seqs, tokens, d), jnp.bfloat16),
            pltpu.VMEM((layers, rank, ff), jnp.bfloat16),
            pltpu.VMEM((layers, rank, d), jnp.bfloat16),
            pltpu.SemaphoreType.DMA((jobs,)),
            pltpu.SemaphoreType.DMA((2,)),
        ],
        compiler_params=pltpu.CompilerParams(vmem_limit_bytes=48 * 2**20),
        name="project",
    )(*[pltpu.with_memory_space_constraint(a, pltpu.HBM) for a in operands])


def product_kernel(scale, own, received, out, square):
    layers, rank = own.shape[0], own.shape[1] // 2
    per_row = 128 // rank
    rows = rank // per_row
    for l in range(layers):
        outer_high, outer_low = pieces(own[l, 0:rank] + received[l, 0:rank])
        inner_high, inner_low = pieces(own[l, rank:] + received[l, rank:])
        both = lax.dot_general(
            jnp.concatenate([outer_high, outer_low], axis=0), inner_high, NT, preferred_element_type=jnp.float32
        )
        third = lax.dot_general(outer_high, inner_low, NT, preferred_element_type=jnp.float32)
        square[l] = (both[0:rank] + (both[rank:] + third)) * scale
        out[l * rows : (l + 1) * rows, :] = jnp.concatenate(
            [square[l, pl.ds(r, rows, stride=per_row), :] for r in range(per_row)], axis=1
        )


def product(own, received):
    layers, double, tokens = own.shape
    rank = double // 2
    return pl.pallas_call(
        functools.partial(product_kernel, tokens ** (-0.5)),
        out_shape=jax.ShapeDtypeStruct((layers * rank * rank // 128, 128), jnp.float32),
        in_specs=[pl.BlockSpec(memory_space=pltpu.VMEM)] * 2,
        out_specs=pl.BlockSpec(memory_space=pltpu.VMEM),
        scratch_shapes=[pltpu.VMEM((layers, rank, rank), jnp.float32)],
        compiler_params=pltpu.CompilerParams(vmem_limit_bytes=4 * 2**20),
        name="product",
    )(own, received)


def gram_kernel(assignment, near, far, seq_grads, fisher):
    total = 2 * near.shape[0]
    local = seq_grads.shape[0]
    tensor, dp = lax.axis_index("tensor"), lax.axis_index("dp")
    core = lax.rem(tensor, 2)
    row_lanes, col_lanes = fisher.shape[0] // 128, fisher.shape[1] // 128

    def block(index, lanes):
        return jnp.concatenate(
            [jnp.concatenate([v[:, index * lanes + r, :] for r in range(lanes)], axis=1) for v in (near, far)], axis=0
        )

    rows, cols = block(dp, row_lanes), block(tensor, col_lanes)
    rows_high, rows_low = pieces(rows)
    cols_high, cols_low = pieces(cols)
    fisher[...] = lax.dot_general(
        jnp.concatenate([rows_high, rows_high, rows_low], axis=0),
        jnp.concatenate([cols_high, cols_low, cols_high], axis=0),
        TN,
        preferred_element_type=jnp.float32,
    ) * (1.0 / total)
    for r in range(local):
        chosen = jnp.zeros((1, cols.shape[1]), jnp.float32)
        for place in range(total):
            slot = lax.bitwise_xor(dp, place % (total // 2)) * 2 + lax.bitwise_xor(core, place // (total // 2))
            chosen = jnp.where(assignment[slot] == dp * local + r, cols[place : place + 1, :], chosen)
        seq_grads[r : r + 1, :] = chosen


def gram(near, far, assignment, local, row_width, col_width):
    return pl.pallas_call(
        gram_kernel,
        out_shape=(
            jax.ShapeDtypeStruct((local, col_width), jnp.float32),
            jax.ShapeDtypeStruct((row_width, col_width), jnp.float32),
        ),
        in_specs=[pl.BlockSpec(memory_space=pltpu.SMEM)] + [pl.BlockSpec(memory_space=pltpu.VMEM)] * 2,
        out_specs=(pl.BlockSpec(memory_space=pltpu.VMEM),) * 2,
        compiler_params=pltpu.CompilerParams(vmem_limit_bytes=8 * 2**20),
        name="gram",
    )(pltpu.with_memory_space_constraint(assignment, pltpu.HBM), near, far)


def swap(value, axis, bit):
    size = lax.axis_size(axis)
    return lax.ppermute(value, axis, [(i, i ^ bit) for i in range(size)])


def two_level(layer_inputs, output_grads, in_proj, out_proj, valid_counts, assignment):
    layers, local = layer_inputs.shape[:2]
    rank = in_proj.shape[2]
    feat = layers * rank * rank
    send, keep = project(layer_inputs, output_grads, in_proj, out_proj, valid_counts)
    chip = keep + swap(send, "tensor", 1)
    vector = product(chip, swap(chip, "tensor", 2))
    gathered = vector[None]
    for bit in (1, 2):
        gathered = jnp.concatenate([gathered, swap(gathered, "dp", bit)], axis=0)
    return gram(gathered, swap(gathered, "tensor", 1), assignment, local, feat // lax.axis_size("dp"), feat // lax.axis_size("tensor"))


def any_sizes(layer_inputs, output_grads, in_proj, out_proj, valid_counts, assignment):
    layers, local, tokens = layer_inputs.shape[:3]
    rank = in_proj.shape[2]
    position = jnp.arange(tokens, dtype=jnp.int32)
    keep = (position[None, :] < valid_counts[:, None]).astype(jnp.float32)
    outer = jnp.einsum("lstd,ldr->lsrt", output_grads, out_proj, preferred_element_type=jnp.float32)
    inner = jnp.einsum("lstf,lfr->lsrt", layer_inputs, in_proj, preferred_element_type=jnp.float32)
    summed = lax.psum(jnp.concatenate([outer, inner * keep[None, :, None, :]], axis=2), "tensor")
    product = jnp.einsum(
        "lsit,lsjt->slij", summed[:, :, :rank], summed[:, :, rank:], precision=lax.Precision.HIGHEST
    )
    vectors = product.reshape(local, layers * rank * rank) * tokens ** (-0.5)
    gathered = lax.all_gather(vectors, "dp", axis=0, tiled=True)
    total, feat = gathered.shape
    dp_index, tensor_index = lax.axis_index("dp"), lax.axis_index("tensor")
    row_width, col_width = feat // lax.axis_size("dp"), feat // lax.axis_size("tensor")
    cols = lax.dynamic_slice_in_dim(gathered, tensor_index * col_width, col_width, 1)
    rows = lax.dynamic_slice_in_dim(gathered, dp_index * row_width, row_width, 1)
    fisher = lax.dot_general(rows, cols, TN, precision=lax.Precision.HIGHEST) / total
    owners = dp_index * local + jnp.arange(local, dtype=jnp.int32)
    selector = (assignment[None, :] == owners[:, None]).astype(jnp.float32)
    return jnp.dot(selector, cols, precision=lax.Precision.HIGHEST), fisher


def on_device(*arrays):
    local = arrays[0].shape[1]
    if lax.axis_size("tensor") == 4 and lax.axis_size("dp") == 4 and local == 2:
        return two_level(*arrays)
    return any_sizes(*arrays)


def solution(mesh):
    return jax.shard_map(
        on_device,
        mesh=mesh,
        in_specs=(
            P(None, ("groups", "dp"), None, "tensor"),
            P(None, ("groups", "dp"), None, "tensor"),
            P(None, "tensor", None),
            P(None, "tensor", None),
            P(("groups", "dp")),
            P("groups"),
        ),
        out_specs=(P(("groups", "dp"), "tensor"), P(("groups", "dp"), "tensor")),
        check_vma=False,
    )
```

```python
import functools

import jax
import jax.numpy as jnp
from jax import lax
from jax.experimental import pallas as pl
from jax.experimental.pallas import tpu as pltpu
from jax.sharding import PartitionSpec as P

NT = (((1,), (1,)), ((), ()))
TN = (((0,), (0,)), ((), ()))


def pieces(value):
    high = value.astype(jnp.bfloat16)
    low = (value - high.astype(jnp.float32)).astype(jnp.bfloat16)
    return high, low


def project_kernel(step, chunks, ahead, counts, x, g, wi, wo, send, keep, xb, gb, wib, wob, sems, wsems):
    layers, rank = wi.shape[0], wi.shape[1]
    tokens = x.shape[2]
    blocks = tokens // step
    core = lax.rem(lax.axis_index("tensor"), 2)
    slots = (1 - core, core)
    valid = [counts[s] for s in slots]
    used = [jnp.clip((v + (step - 1)) // step, 1, blocks) for v in valid]
    pairs = ((x, xb, wi, wib), (g, gb, wo, wob))
    jobs = [
        (which, j, l, k, width)
        for j in range(2)
        for l in range(layers)
        for which in range(2)
        for k, width in chunks(which, j, l)
    ]
    started = []
    for i in range(len(jobs)):
        n = max(i + 1, started[-1] if started else 0)
        while n < len(jobs) and sum(job[4] for job in jobs[i + 1 : n]) < ahead:
            n += 1
        started.append(n)

    def copy(i, n):
        which, j, l, k, width = jobs[i]
        src, dst = pairs[which][:2]
        rows, cols = pl.ds(0, n), pl.ds(k, width)
        return pltpu.make_async_copy(src.at[l, slots[j], rows, cols], dst.at[l, j, rows, cols], sems.at[i])

    def weight_copy(which, l):
        src, dst = pairs[which][2:]
        return pltpu.make_async_copy(src.at[l], dst.at[l], wsems.at[which * layers + l])

    def start(i):
        which, j, l, k, _ = jobs[i]
        if j == 0 and k == 0:
            weight_copy(which, l).start()
        copy(i, pl.multiple_of(used[j] * step, step)).start()

    def job(i, n):
        which, j, l, k, width = jobs[i]
        for n_next in range(started[i - 1] if i else started[0], started[i]):
            start(n_next)
        if j == 0 and k == 0:
            weight_copy(which, l).wait()
        copy(i, n).wait()
        _, data, _, weight = pairs[which]
        out = (send, keep)[j]
        rows = pl.ds((rank, 0)[which], rank)
        w = weight[l, :, k : k + width]
        cut = n - n // (2 * step) * step
        d = lax.dot_general(w, data[l, j, 0:cut, k : k + width], NT, preferred_element_type=jnp.float32)
        if cut < n:
            other = lax.dot_general(data[l, j, cut:n, k : k + width], w, NT, preferred_element_type=jnp.float32)
            d = jnp.concatenate([d, other.T], axis=1)
        if k > 0:
            d = d + out[l, rows, 0:n]
        if which == 0 and k + width == data.shape[3]:
            d = jnp.where(lax.broadcasted_iota(jnp.int32, (rank, n), 1) < valid[j], d, 0.0)
        out[l, rows, 0:n] = d

    for i in range(started[0]):
        start(i)
    send[...] = jnp.zeros_like(send)
    keep[...] = jnp.zeros_like(keep)
    half = sum(job[1] == 0 for job in jobs)
    for j in range(2):
        for v in range(1, blocks + 1):

            @pl.when(used[j] == v)
            def _():
                for i in (range(half), range(half, len(jobs)))[j]:
                    pl.when(valid[j] >= -i)(functools.partial(job, i, step * v))


def project(layer_inputs, output_grads, in_proj, out_proj, valid_counts):
    layers, seqs, tokens, ff = layer_inputs.shape
    d = output_grads.shape[3]
    rank = in_proj.shape[2]
    def chunks(which, j, l):
        parts = ([ff - ff // 2, ff // 2], [d])[which]
        if (which, j, l) == (0, 0, 0):
            parts = [ff // 7, ff // 7, parts[0] - 2 * (ff // 7), parts[1]]
        return [(sum(parts[:i]), part) for i, part in enumerate(parts)]

    jobs = sum(len(chunks(which, j, l)) for which in range(2) for j in range(2) for l in range(layers))
    anywhere = pl.BlockSpec(memory_space=pl.ANY)
    out = pltpu.VMEM((layers, 2 * rank, tokens), jnp.float32)
    operands = (valid_counts, layer_inputs, output_grads, jnp.swapaxes(in_proj, 1, 2), jnp.swapaxes(out_proj, 1, 2))
    return pl.pallas_call(
        functools.partial(project_kernel, tokens // 4, chunks, 3 * ff // 2),
        out_shape=(out, out),
        in_specs=[pl.BlockSpec(memory_space=pltpu.SMEM)] + [anywhere] * 4,
        out_specs=(pl.BlockSpec(memory_space=pltpu.VMEM),) * 2,
        scratch_shapes=[
            pltpu.VMEM((layers, seqs, tokens, ff), jnp.bfloat16),
            pltpu.VMEM((layers, seqs, tokens, d), jnp.bfloat16),
            pltpu.VMEM((layers, rank, ff), jnp.bfloat16),
            pltpu.VMEM((layers, rank, d), jnp.bfloat16),
            pltpu.SemaphoreType.DMA((jobs,)),
            pltpu.SemaphoreType.DMA((2 * layers,)),
        ],
        compiler_params=pltpu.CompilerParams(vmem_limit_bytes=48 * 2**20),
        name="project",
    )(*[pltpu.with_memory_space_constraint(a, pltpu.HBM) for a in operands])


def product_kernel(scale, own, received, out, square):
    layers, rank = own.shape[0], own.shape[1] // 2
    per_row = 128 // rank
    rows = rank // per_row
    for l in range(layers):
        outer_high, outer_low = pieces(own[l, 0:rank] + received[l, 0:rank])
        inner_high, inner_low = pieces(own[l, rank:] + received[l, rank:])
        both = lax.dot_general(
            jnp.concatenate([outer_high, outer_low], axis=0), inner_high, NT, preferred_element_type=jnp.float32
        )
        third = lax.dot_general(outer_high, inner_low, NT, preferred_element_type=jnp.float32)
        square[l] = (both[0:rank] + (both[rank:] + third)) * scale
        out[l * rows : (l + 1) * rows, :] = jnp.concatenate(
            [square[l, pl.ds(r, rows, stride=per_row), :] for r in range(per_row)], axis=1
        )


def product(own, received):
    layers, double, tokens = own.shape
    rank = double // 2
    return pl.pallas_call(
        functools.partial(product_kernel, tokens ** (-0.5)),
        out_shape=jax.ShapeDtypeStruct((layers * rank * rank // 128, 128), jnp.float32),
        in_specs=[pl.BlockSpec(memory_space=pltpu.VMEM)] * 2,
        out_specs=pl.BlockSpec(memory_space=pltpu.VMEM),
        scratch_shapes=[pltpu.VMEM((layers, rank, rank), jnp.float32)],
        compiler_params=pltpu.CompilerParams(vmem_limit_bytes=4 * 2**20),
        name="product",
    )(own, received)


def gram_kernel(assignment, own, received, seq_grads, fisher, slots, chosen, block, sems):
    total = 2 * own.shape[0]
    local = chosen.shape[0]
    tensor, dp = lax.axis_index("tensor"), lax.axis_index("dp")
    core = lax.rem(tensor, 2)
    row_lanes, col_lanes = block.shape[0] // 128, block.shape[1] // 128
    fetch = pltpu.make_async_copy(assignment, slots, sems.at[0])
    fetch.start()

    def lanes(index, count):
        return jnp.concatenate(
            [
                jnp.concatenate([v[:, index * count + r, :] for r in range(count)], axis=1)
                for v in (own, received)
            ],
            axis=0,
        )

    rows = lanes(dp, row_lanes) * (1.0 / total)
    cols = lanes(tensor, col_lanes)
    rows_high, rows_low = pieces(rows)
    cols_high, cols_low = pieces(cols)
    left = jnp.concatenate([rows_high, rows_high, rows_low], axis=0)
    right = jnp.concatenate([cols_high, cols_low, cols_high], axis=0)
    copies = []
    steps = 2
    height = block.shape[0] // steps
    for i in range(steps):
        part = pl.ds(i * height, height)
        block[part, :] = lax.dot_general(
            left[:, i * height : (i + 1) * height], right, TN, preferred_element_type=jnp.float32
        )
        copies.append(pltpu.make_async_copy(block.at[part, :], fisher.at[part, :], sems.at[1 + i]))
        copies[-1].start()
    fetch.wait()
    for r in range(local):
        picked = jnp.zeros((1, cols.shape[1]), jnp.float32)
        for place in range(total):
            slot = lax.bitwise_xor(dp, place % (total // 2)) * 2 + lax.bitwise_xor(core, place // (total // 2))
            picked = jnp.where(slots[slot] == dp * local + r, cols[place : place + 1, :], picked)
        chosen[r : r + 1, :] = picked
    copies.append(pltpu.make_async_copy(chosen, seq_grads, sems.at[1 + steps]))
    copies[-1].start()
    for c in copies:
        c.wait()


def gram(own, received, assignment, local, row_width, col_width):
    anywhere = pl.BlockSpec(memory_space=pl.ANY)
    return pl.pallas_call(
        gram_kernel,
        out_shape=(
            jax.ShapeDtypeStruct((local, col_width), jnp.float32),
            jax.ShapeDtypeStruct((row_width, col_width), jnp.float32),
        ),
        in_specs=[anywhere] + [pl.BlockSpec(memory_space=pltpu.VMEM)] * 2,
        out_specs=(anywhere,) * 2,
        scratch_shapes=[
            pltpu.SMEM(assignment.shape, jnp.int32),
            pltpu.VMEM((local, col_width), jnp.float32),
            pltpu.VMEM((row_width, col_width), jnp.float32),
            pltpu.SemaphoreType.DMA((4,)),
        ],
        compiler_params=pltpu.CompilerParams(vmem_limit_bytes=8 * 2**20),
        name="gram",
    )(pltpu.with_memory_space_constraint(assignment, pltpu.HBM), own, received)


def swap(value, axis, bit):
    size = lax.axis_size(axis)
    return lax.ppermute(value, axis, [(i, i ^ bit) for i in range(size)])


def two_level(layer_inputs, output_grads, in_proj, out_proj, valid_counts, assignment):
    layers, local = layer_inputs.shape[:2]
    rank = in_proj.shape[2]
    feat = layers * rank * rank
    send, keep = project(layer_inputs, output_grads, in_proj, out_proj, valid_counts)
    chip = keep + swap(send, "tensor", 1)
    vector = product(chip, swap(chip, "tensor", 2))
    gathered = vector[None]
    for bit in (1, 2):
        gathered = jnp.concatenate([gathered, swap(gathered, "dp", bit)], axis=0)
    return gram(gathered, swap(gathered, "tensor", 1), assignment, local, feat // lax.axis_size("dp"), feat // lax.axis_size("tensor"))


def any_sizes(layer_inputs, output_grads, in_proj, out_proj, valid_counts, assignment):
    layers, local, tokens = layer_inputs.shape[:3]
    rank = in_proj.shape[2]
    position = jnp.arange(tokens, dtype=jnp.int32)
    keep = (position[None, :] < valid_counts[:, None]).astype(jnp.float32)
    outer = jnp.einsum("lstd,ldr->lsrt", output_grads, out_proj, preferred_element_type=jnp.float32)
    inner = jnp.einsum("lstf,lfr->lsrt", layer_inputs, in_proj, preferred_element_type=jnp.float32)
    summed = lax.psum(jnp.concatenate([outer, inner * keep[None, :, None, :]], axis=2), "tensor")
    product = jnp.einsum(
        "lsit,lsjt->slij", summed[:, :, :rank], summed[:, :, rank:], precision=lax.Precision.HIGHEST
    )
    vectors = product.reshape(local, layers * rank * rank) * tokens ** (-0.5)
    gathered = lax.all_gather(vectors, "dp", axis=0, tiled=True)
    total, feat = gathered.shape
    dp_index, tensor_index = lax.axis_index("dp"), lax.axis_index("tensor")
    row_width, col_width = feat // lax.axis_size("dp"), feat // lax.axis_size("tensor")
    cols = lax.dynamic_slice_in_dim(gathered, tensor_index * col_width, col_width, 1)
    rows = lax.dynamic_slice_in_dim(gathered, dp_index * row_width, row_width, 1)
    fisher = lax.dot_general(rows, cols, TN, precision=lax.Precision.HIGHEST) / total
    owners = dp_index * local + jnp.arange(local, dtype=jnp.int32)
    selector = (assignment[None, :] == owners[:, None]).astype(jnp.float32)
    return jnp.dot(selector, cols, precision=lax.Precision.HIGHEST), fisher


def on_device(*arrays):
    local = arrays[0].shape[1]
    if lax.axis_size("tensor") == 4 and lax.axis_size("dp") == 4 and local == 2:
        return two_level(*arrays)
    return any_sizes(*arrays)


def solution(mesh):
    return jax.shard_map(
        on_device,
        mesh=mesh,
        in_specs=(
            P(None, ("groups", "dp"), None, "tensor"),
            P(None, ("groups", "dp"), None, "tensor"),
            P(None, "tensor", None),
            P(None, "tensor", None),
            P(("groups", "dp")),
            P("groups"),
        ),
        out_specs=(P(("groups", "dp"), "tensor"), P(("groups", "dp"), "tensor")),
        check_vma=False,
    )
```

```python
import functools

import jax
import jax.numpy as jnp
from jax import lax
from jax.experimental import pallas as pl
from jax.experimental.pallas import tpu as pltpu
from jax.sharding import PartitionSpec as P

NT = (((1,), (1,)), ((), ()))
TN = (((0,), (0,)), ((), ()))


def pieces(value):
    high = value.astype(jnp.bfloat16)
    low = (value - high.astype(jnp.float32)).astype(jnp.bfloat16)
    return high, low


def project_kernel(step, chunks, ahead, counts, x, g, wi, wo, send, keep, xb, gb, wib, wob, sems, wsems):
    layers, rank = wi.shape[0], wi.shape[1]
    tokens = x.shape[2]
    blocks = tokens // step
    core = lax.rem(lax.axis_index("tensor"), 2)
    slots = (1 - core, core)
    valid = [counts[s] for s in slots]
    used = [jnp.clip((v + (step - 1)) // step, 1, blocks) for v in valid]
    pairs = ((x, xb, wi, wib), (g, gb, wo, wob))
    jobs = [
        (which, j, l, k, width)
        for j in range(2)
        for l in range(layers)
        for which in range(2)
        for k, width in chunks(which, j, l)
    ]
    started = []
    for i in range(len(jobs)):
        n = max(i + 1, started[-1] if started else 0)
        while n < len(jobs) and sum(job[4] for job in jobs[i + 1 : n]) < ahead:
            n += 1
        started.append(n)

    def copy(i, n):
        which, j, l, k, width = jobs[i]
        src, dst = pairs[which][:2]
        rows, cols = pl.ds(0, n), pl.ds(k, width)
        return pltpu.make_async_copy(src.at[l, slots[j], rows, cols], dst.at[l, j, rows, cols], sems.at[i])

    def weight_copy(which, l):
        src, dst = pairs[which][2:]
        return pltpu.make_async_copy(src.at[l], dst.at[l], wsems.at[which * layers + l])

    def start(i):
        which, j, l, k, _ = jobs[i]
        if j == 0 and k == 0:
            weight_copy(which, l).start()
        copy(i, pl.multiple_of(used[j] * step, step)).start()

    def job(i, n):
        which, j, l, k, width = jobs[i]
        for n_next in range(started[i - 1] if i else started[0], started[i]):
            start(n_next)
        if j == 0 and k == 0:
            weight_copy(which, l).wait()
        copy(i, n).wait()
        _, data, _, weight = pairs[which]
        out = (send, keep)[j]
        rows = pl.ds((rank, 0)[which], rank)
        w = weight[l, :, k : k + width]
        cut = n - n // (2 * step) * step
        d = lax.dot_general(w, data[l, j, 0:cut, k : k + width], NT, preferred_element_type=jnp.float32)
        if cut < n:
            other = lax.dot_general(data[l, j, cut:n, k : k + width], w, NT, preferred_element_type=jnp.float32)
            d = jnp.concatenate([d, other.T], axis=1)
        if k > 0:
            d = d + out[l, rows, 0:n]
        if which == 0 and k + width == data.shape[3]:
            d = jnp.where(lax.broadcasted_iota(jnp.int32, (rank, n), 1) < valid[j], d, 0.0)
        out[l, rows, 0:n] = d

    for i in range(started[0]):
        start(i)
    send[...] = jnp.zeros_like(send)
    keep[...] = jnp.zeros_like(keep)
    half = sum(job[1] == 0 for job in jobs)
    for j in range(2):
        for v in range(1, blocks + 1):

            @pl.when(used[j] == v)
            def _():
                for i in (range(half), range(half, len(jobs)))[j]:
                    pl.when(valid[j] >= -i)(functools.partial(job, i, step * v))


def project(layer_inputs, output_grads, in_proj, out_proj, valid_counts):
    layers, seqs, tokens, ff = layer_inputs.shape
    d = output_grads.shape[3]
    rank = in_proj.shape[2]
    def chunks(which, j, l):
        parts = ([ff - ff // 2, ff // 2], [d])[which]
        if (which, j, l) == (0, 0, 0):
            parts = [ff // 7, ff // 7, parts[0] - 2 * (ff // 7), parts[1]]
        return [(sum(parts[:i]), part) for i, part in enumerate(parts)]

    jobs = sum(len(chunks(which, j, l)) for which in range(2) for j in range(2) for l in range(layers))
    anywhere = pl.BlockSpec(memory_space=pl.ANY)
    out = pltpu.VMEM((layers, 2 * rank, tokens), jnp.float32)
    operands = (valid_counts, layer_inputs, output_grads, jnp.swapaxes(in_proj, 1, 2), jnp.swapaxes(out_proj, 1, 2))
    return pl.pallas_call(
        functools.partial(project_kernel, tokens // 4, chunks, 3 * ff // 2),
        out_shape=(out, out),
        in_specs=[pl.BlockSpec(memory_space=pltpu.SMEM)] + [anywhere] * 4,
        out_specs=(pl.BlockSpec(memory_space=pltpu.VMEM),) * 2,
        scratch_shapes=[
            pltpu.VMEM((layers, seqs, tokens, ff), jnp.bfloat16),
            pltpu.VMEM((layers, seqs, tokens, d), jnp.bfloat16),
            pltpu.VMEM((layers, rank, ff), jnp.bfloat16),
            pltpu.VMEM((layers, rank, d), jnp.bfloat16),
            pltpu.SemaphoreType.DMA((jobs,)),
            pltpu.SemaphoreType.DMA((2 * layers,)),
        ],
        compiler_params=pltpu.CompilerParams(vmem_limit_bytes=48 * 2**20),
        name="project",
    )(*[pltpu.with_memory_space_constraint(a, pltpu.HBM) for a in operands])


def product_kernel(scale, own, received, out, square):
    layers, rank = own.shape[0], own.shape[1] // 2
    per_row = 128 // rank
    rows = rank // per_row
    for l in range(layers):
        outer_high, outer_low = pieces(own[l, 0:rank] + received[l, 0:rank])
        inner_high, inner_low = pieces(own[l, rank:] + received[l, rank:])
        both = lax.dot_general(
            jnp.concatenate([outer_high, outer_low], axis=0), inner_high, NT, preferred_element_type=jnp.float32
        )
        third = lax.dot_general(outer_high, inner_low, NT, preferred_element_type=jnp.float32)
        square[l] = (both[0:rank] + (both[rank:] + third)) * scale
        out[l * rows : (l + 1) * rows, :] = jnp.concatenate(
            [square[l, pl.ds(r, rows, stride=per_row), :] for r in range(per_row)], axis=1
        )


def product(own, received):
    layers, double, tokens = own.shape
    rank = double // 2
    return pl.pallas_call(
        functools.partial(product_kernel, tokens ** (-0.5)),
        out_shape=jax.ShapeDtypeStruct((layers * rank * rank // 128, 128), jnp.float32),
        in_specs=[pl.BlockSpec(memory_space=pltpu.VMEM)] * 2,
        out_specs=pl.BlockSpec(memory_space=pltpu.VMEM),
        scratch_shapes=[pltpu.VMEM((layers, rank, rank), jnp.float32)],
        compiler_params=pltpu.CompilerParams(vmem_limit_bytes=4 * 2**20),
        name="product",
    )(own, received)


def gram_kernel(assignment, own, one, two, three, seq_grads, fisher, slots, chosen, block, sems):
    total = 4 * own.shape[0]
    local = chosen.shape[0]
    tensor, dp = lax.axis_index("tensor"), lax.axis_index("dp")
    core = lax.rem(tensor, 2)
    row_lanes, col_lanes = block.shape[0] // 128, block.shape[1] // 128
    fetch = pltpu.make_async_copy(assignment, slots, sems.at[0])
    fetch.start()

    def lanes(index, count):
        return jnp.concatenate(
            [
                jnp.concatenate([v[:, index * count + r, :] for r in range(count)], axis=1)
                for v in (own, one, two, three)
            ],
            axis=0,
        )

    rows = lanes(dp, row_lanes) * (1.0 / total)
    cols = lanes(tensor, col_lanes)
    rows_high, rows_low = pieces(rows)
    cols_high, cols_low = pieces(cols)
    left = jnp.concatenate([rows_high, rows_high, rows_low], axis=0)
    right = jnp.concatenate([cols_high, cols_low, cols_high], axis=0)
    copies = []
    steps = 2
    height = block.shape[0] // steps
    for i in range(steps):
        part = pl.ds(i * height, height)
        block[part, :] = lax.dot_general(
            left[:, i * height : (i + 1) * height], right, TN, preferred_element_type=jnp.float32
        )
        copies.append(pltpu.make_async_copy(block.at[part, :], fisher.at[part, :], sems.at[1 + i]))
        copies[-1].start()
    fetch.wait()
    for r in range(local):
        picked = jnp.zeros((1, cols.shape[1]), jnp.float32)
        for place in range(total):
            slot = lax.bitwise_xor(dp, place // 2) * 2 + lax.bitwise_xor(core, place % 2)
            picked = jnp.where(slots[slot] == dp * local + r, cols[place : place + 1, :], picked)
        chosen[r : r + 1, :] = picked
    copies.append(pltpu.make_async_copy(chosen, seq_grads, sems.at[1 + steps]))
    copies[-1].start()
    for c in copies:
        c.wait()


def gram(vectors, assignment, local, row_width, col_width):
    anywhere = pl.BlockSpec(memory_space=pl.ANY)
    return pl.pallas_call(
        gram_kernel,
        out_shape=(
            jax.ShapeDtypeStruct((local, col_width), jnp.float32),
            jax.ShapeDtypeStruct((row_width, col_width), jnp.float32),
        ),
        in_specs=[anywhere] + [pl.BlockSpec(memory_space=pltpu.VMEM)] * 4,
        out_specs=(anywhere,) * 2,
        scratch_shapes=[
            pltpu.SMEM(assignment.shape, jnp.int32),
            pltpu.VMEM((local, col_width), jnp.float32),
            pltpu.VMEM((row_width, col_width), jnp.float32),
            pltpu.SemaphoreType.DMA((4,)),
        ],
        compiler_params=pltpu.CompilerParams(vmem_limit_bytes=8 * 2**20),
        name="gram",
    )(pltpu.with_memory_space_constraint(assignment, pltpu.HBM), *vectors)


def swap(value, axis, bit):
    size = lax.axis_size(axis)
    return lax.ppermute(value, axis, [(i, i ^ bit) for i in range(size)])


def two_level(layer_inputs, output_grads, in_proj, out_proj, valid_counts, assignment):
    layers, local = layer_inputs.shape[:2]
    rank = in_proj.shape[2]
    feat = layers * rank * rank
    send, keep = project(layer_inputs, output_grads, in_proj, out_proj, valid_counts)
    chip = keep + swap(send, "tensor", 1)
    vector = product(chip, swap(chip, "tensor", 2))
    pair = jnp.stack([vector, swap(vector, "tensor", 1)])
    parts = [swap(pair, "dp", bit) for bit in (1, 2, 3)]
    return gram([pair] + parts, assignment, local, feat // lax.axis_size("dp"), feat // lax.axis_size("tensor"))


def any_sizes(layer_inputs, output_grads, in_proj, out_proj, valid_counts, assignment):
    layers, local, tokens = layer_inputs.shape[:3]
    rank = in_proj.shape[2]
    position = jnp.arange(tokens, dtype=jnp.int32)
    keep = (position[None, :] < valid_counts[:, None]).astype(jnp.float32)
    outer = jnp.einsum("lstd,ldr->lsrt", output_grads, out_proj, preferred_element_type=jnp.float32)
    inner = jnp.einsum("lstf,lfr->lsrt", layer_inputs, in_proj, preferred_element_type=jnp.float32)
    summed = lax.psum(jnp.concatenate([outer, inner * keep[None, :, None, :]], axis=2), "tensor")
    product = jnp.einsum(
        "lsit,lsjt->slij", summed[:, :, :rank], summed[:, :, rank:], precision=lax.Precision.HIGHEST
    )
    vectors = product.reshape(local, layers * rank * rank) * tokens ** (-0.5)
    gathered = lax.all_gather(vectors, "dp", axis=0, tiled=True)
    total, feat = gathered.shape
    dp_index, tensor_index = lax.axis_index("dp"), lax.axis_index("tensor")
    row_width, col_width = feat // lax.axis_size("dp"), feat // lax.axis_size("tensor")
    cols = lax.dynamic_slice_in_dim(gathered, tensor_index * col_width, col_width, 1)
    rows = lax.dynamic_slice_in_dim(gathered, dp_index * row_width, row_width, 1)
    fisher = lax.dot_general(rows, cols, TN, precision=lax.Precision.HIGHEST) / total
    owners = dp_index * local + jnp.arange(local, dtype=jnp.int32)
    selector = (assignment[None, :] == owners[:, None]).astype(jnp.float32)
    return jnp.dot(selector, cols, precision=lax.Precision.HIGHEST), fisher


def on_device(*arrays):
    local = arrays[0].shape[1]
    if lax.axis_size("tensor") == 4 and lax.axis_size("dp") == 4 and local == 2:
        return two_level(*arrays)
    return any_sizes(*arrays)


def solution(mesh):
    return jax.shard_map(
        on_device,
        mesh=mesh,
        in_specs=(
            P(None, ("groups", "dp"), None, "tensor"),
            P(None, ("groups", "dp"), None, "tensor"),
            P(None, "tensor", None),
            P(None, "tensor", None),
            P(("groups", "dp")),
            P("groups"),
        ),
        out_specs=(P(("groups", "dp"), "tensor"), P(("groups", "dp"), "tensor")),
        check_vma=False,
    )
```

```python
import functools

import jax
import jax.numpy as jnp
from jax import lax
from jax.experimental import pallas as pl
from jax.experimental.pallas import tpu as pltpu
from jax.sharding import PartitionSpec as P

NT = (((1,), (1,)), ((), ()))
TN = (((0,), (0,)), ((), ()))


def pieces(value):
    high = value.astype(jnp.bfloat16)
    low = (value - high.astype(jnp.float32)).astype(jnp.bfloat16)
    return high, low


def project_kernel(step, chunks, ahead, counts, x, g, wi, wo, *refs):
    layers = wi.shape[0]
    send, keep = refs[:layers], refs[layers : 2 * layers]
    xb, gb, wib, wob, sems, wsems = refs[2 * layers :]
    layers, rank = wi.shape[0], wi.shape[1]
    tokens = x.shape[2]
    blocks = tokens // step
    core = lax.rem(lax.axis_index("tensor"), 2)
    slots = (1 - core, core)
    valid = [counts[s] for s in slots]
    used = [jnp.clip((v + (step - 1)) // step, 1, blocks) for v in valid]
    fetched = [pl.multiple_of(jnp.clip((v + 15) // 16, 1, tokens // 16) * 16, 16) for v in valid]
    pairs = ((x, xb, wi, wib), (g, gb, wo, wob))
    jobs = [
        (which, j, l, k, width)
        for j in range(2)
        for l in range(layers)
        for which in range(2)
        for k, width in chunks(which, j, l)
    ]
    started = []
    for i in range(len(jobs)):
        n = max(i + 1, started[-1] if started else 0)
        while n < len(jobs) and sum(job[4] for job in jobs[i + 1 : n]) < ahead:
            n += 1
        started.append(n)

    def copy(i, n):
        which, j, l, k, width = jobs[i]
        src, dst = pairs[which][:2]
        rows, cols = pl.ds(0, n), pl.ds(k, width)
        return pltpu.make_async_copy(src.at[l, slots[j], rows, cols], dst.at[l, j, rows, cols], sems.at[i])

    def weight_copy(which, l):
        src, dst = pairs[which][2:]
        return pltpu.make_async_copy(src.at[l], dst.at[l], wsems.at[which * layers + l])

    def start(i):
        which, j, l, k, _ = jobs[i]
        if j == 0 and k == 0:
            weight_copy(which, l).start()
        copy(i, fetched[j]).start()

    def job(i, n):
        which, j, l, k, width = jobs[i]
        for n_next in range(started[i - 1] if i else started[0], started[i]):
            start(n_next)
        if j == 0 and k == 0:
            weight_copy(which, l).wait()
        copy(i, fetched[j]).wait()
        _, data, _, weight = pairs[which]
        out = (send, keep)[j][l]
        rows = pl.ds((rank, 0)[which], rank)
        w = weight[l, :, k : k + width]
        cut = n - n // (2 * step) * step
        d = lax.dot_general(w, data[l, j, 0:cut, k : k + width], NT, preferred_element_type=jnp.float32)
        if cut < n:
            other = lax.dot_general(data[l, j, cut:n, k : k + width], w, NT, preferred_element_type=jnp.float32)
            d = jnp.concatenate([d, other.T], axis=1)
        if k > 0:
            d = d + out[rows, 0:n]
        if k + width == data.shape[3]:
            d = jnp.where(lax.broadcasted_iota(jnp.int32, (rank, n), 1) < valid[j], d, 0.0)
        out[rows, 0:n] = d

    for i in range(started[0]):
        start(i)
    for ref in send + keep:
        ref[...] = jnp.zeros_like(ref)
    half = sum(job[1] == 0 for job in jobs)
    for j in range(2):
        for v in range(1, blocks + 1):

            @pl.when(used[j] == v)
            def _():
                for i in (range(half), range(half, len(jobs)))[j]:
                    pl.when(valid[j] >= -i)(functools.partial(job, i, step * v))


def project(layer_inputs, output_grads, in_proj, out_proj, valid_counts):
    layers, seqs, tokens, ff = layer_inputs.shape
    d = output_grads.shape[3]
    rank = in_proj.shape[2]
    def chunks(which, j, l):
        parts = ([ff - ff // 2, ff // 2], [d])[which]
        if (which, j, l) == (0, 0, 0):
            parts = [ff // 7, ff // 7, parts[0] - 2 * (ff // 7), parts[1]]
        return [(sum(parts[:i]), part) for i, part in enumerate(parts)]

    jobs = sum(len(chunks(which, j, l)) for which in range(2) for j in range(2) for l in range(layers))
    anywhere = pl.BlockSpec(memory_space=pl.ANY)
    out = pltpu.VMEM((2 * rank, tokens), jnp.float32)
    operands = (valid_counts, layer_inputs, output_grads, jnp.swapaxes(in_proj, 1, 2), jnp.swapaxes(out_proj, 1, 2))
    outs = pl.pallas_call(
        functools.partial(project_kernel, tokens // 4, chunks, 2 * ff),
        out_shape=(out,) * (2 * layers),
        in_specs=[pl.BlockSpec(memory_space=pltpu.SMEM)] + [anywhere] * 4,
        out_specs=(pl.BlockSpec(memory_space=pltpu.VMEM),) * (2 * layers),
        scratch_shapes=[
            pltpu.VMEM((layers, seqs, tokens, ff), jnp.bfloat16),
            pltpu.VMEM((layers, seqs, tokens, d), jnp.bfloat16),
            pltpu.VMEM((layers, rank, ff), jnp.bfloat16),
            pltpu.VMEM((layers, rank, d), jnp.bfloat16),
            pltpu.SemaphoreType.DMA((jobs,)),
            pltpu.SemaphoreType.DMA((2 * layers,)),
        ],
        compiler_params=pltpu.CompilerParams(vmem_limit_bytes=48 * 2**20),
        name="project",
    )(*[pltpu.with_memory_space_constraint(a, pltpu.HBM) for a in operands])
    return outs[:layers], outs[layers:]


def product_kernel(scale, *refs):
    out, square = refs[-2:]
    layers = square.shape[0]
    rank = square.shape[1]
    per_row = 128 // rank
    rows = rank // per_row
    for l in range(layers):
        own, received = refs[l], refs[layers + l]
        outer_high, outer_low = pieces(own[0:rank] + received[0:rank])
        inner_high, inner_low = pieces(own[rank:] + received[rank:])
        both = lax.dot_general(
            jnp.concatenate([outer_high, outer_low], axis=0), inner_high, NT, preferred_element_type=jnp.float32
        )
        third = lax.dot_general(outer_high, inner_low, NT, preferred_element_type=jnp.float32)
        square[l] = (both[0:rank] + (both[rank:] + third)) * scale
        out[l * rows : (l + 1) * rows, :] = jnp.concatenate(
            [square[l, pl.ds(r, rows, stride=per_row), :] for r in range(per_row)], axis=1
        )


def product(own, received):
    layers = len(own)
    double, tokens = own[0].shape
    rank = double // 2
    return pl.pallas_call(
        functools.partial(product_kernel, tokens ** (-0.5)),
        out_shape=jax.ShapeDtypeStruct((layers * rank * rank // 128, 128), jnp.float32),
        in_specs=[pl.BlockSpec(memory_space=pltpu.VMEM)] * (2 * layers),
        out_specs=pl.BlockSpec(memory_space=pltpu.VMEM),
        scratch_shapes=[pltpu.VMEM((layers, rank, rank), jnp.float32)],
        compiler_params=pltpu.CompilerParams(vmem_limit_bytes=4 * 2**20),
        name="product",
    )(*own, *received)


def gram_kernel(assignment, own, one, two, three, seq_grads, fisher, slots, chosen, block, sems):
    total = 4 * own.shape[0]
    local = chosen.shape[0]
    tensor, dp = lax.axis_index("tensor"), lax.axis_index("dp")
    core = lax.rem(tensor, 2)
    row_lanes, col_lanes = block.shape[0] // 128, block.shape[1] // 128
    fetch = pltpu.make_async_copy(assignment, slots, sems.at[0])
    fetch.start()

    def lanes(index, count):
        return jnp.concatenate(
            [
                jnp.concatenate([v[:, index * count + r, :] for r in range(count)], axis=1)
                for v in (own, one, two, three)
            ],
            axis=0,
        )

    rows = lanes(dp, row_lanes) * (1.0 / total)
    cols = lanes(tensor, col_lanes)
    rows_high, rows_low = pieces(rows)
    cols_high, cols_low = pieces(cols)
    left = jnp.concatenate([rows_high, rows_high, rows_low], axis=0)
    right = jnp.concatenate([cols_high, cols_low, cols_high], axis=0)
    copies = []
    steps = 2
    height = block.shape[0] // steps
    for i in range(steps):
        part = pl.ds(i * height, height)
        block[part, :] = lax.dot_general(
            left[:, i * height : (i + 1) * height], right, TN, preferred_element_type=jnp.float32
        )
        copies.append(pltpu.make_async_copy(block.at[part, :], fisher.at[part, :], sems.at[1 + i]))
        copies[-1].start()
    fetch.wait()
    for r in range(local):
        picked = jnp.zeros((1, cols.shape[1]), jnp.float32)
        for place in range(total):
            slot = lax.bitwise_xor(dp, place // 2) * 2 + lax.bitwise_xor(core, place % 2)
            picked = jnp.where(slots[slot] == dp * local + r, cols[place : place + 1, :], picked)
        chosen[r : r + 1, :] = picked
    copies.append(pltpu.make_async_copy(chosen, seq_grads, sems.at[1 + steps]))
    copies[-1].start()
    for c in copies:
        c.wait()


def gram(vectors, assignment, local, row_width, col_width):
    anywhere = pl.BlockSpec(memory_space=pl.ANY)
    return pl.pallas_call(
        gram_kernel,
        out_shape=(
            jax.ShapeDtypeStruct((local, col_width), jnp.float32),
            jax.ShapeDtypeStruct((row_width, col_width), jnp.float32),
        ),
        in_specs=[anywhere] + [pl.BlockSpec(memory_space=pltpu.VMEM)] * 4,
        out_specs=(anywhere,) * 2,
        scratch_shapes=[
            pltpu.SMEM(assignment.shape, jnp.int32),
            pltpu.VMEM((local, col_width), jnp.float32),
            pltpu.VMEM((row_width, col_width), jnp.float32),
            pltpu.SemaphoreType.DMA((4,)),
        ],
        compiler_params=pltpu.CompilerParams(vmem_limit_bytes=8 * 2**20),
        name="gram",
    )(pltpu.with_memory_space_constraint(assignment, pltpu.HBM), *vectors)


def swap(value, axis, bit):
    size = lax.axis_size(axis)
    return lax.ppermute(value, axis, [(i, i ^ bit) for i in range(size)])


def two_level(layer_inputs, output_grads, in_proj, out_proj, valid_counts, assignment):
    layers, local = layer_inputs.shape[:2]
    rank = in_proj.shape[2]
    feat = layers * rank * rank
    send, keep = project(layer_inputs, output_grads, in_proj, out_proj, valid_counts)
    chip = [keep[l] + swap(send[l], "tensor", 1) for l in range(layers)]
    received = [swap(c, "tensor", 2) for c in chip]
    vector = product(chip, received)
    pair = jnp.stack([vector, swap(vector, "tensor", 1)])
    parts = [swap(pair, "dp", bit) for bit in (1, 2, 3)]
    return gram([pair] + parts, assignment, local, feat // lax.axis_size("dp"), feat // lax.axis_size("tensor"))


def any_sizes(layer_inputs, output_grads, in_proj, out_proj, valid_counts, assignment):
    layers, local, tokens = layer_inputs.shape[:3]
    rank = in_proj.shape[2]
    position = jnp.arange(tokens, dtype=jnp.int32)
    keep = (position[None, :] < valid_counts[:, None]).astype(jnp.float32)
    outer = jnp.einsum("lstd,ldr->lsrt", output_grads, out_proj, preferred_element_type=jnp.float32)
    inner = jnp.einsum("lstf,lfr->lsrt", layer_inputs, in_proj, preferred_element_type=jnp.float32)
    summed = lax.psum(jnp.concatenate([outer, inner * keep[None, :, None, :]], axis=2), "tensor")
    product = jnp.einsum(
        "lsit,lsjt->slij", summed[:, :, :rank], summed[:, :, rank:], precision=lax.Precision.HIGHEST
    )
    vectors = product.reshape(local, layers * rank * rank) * tokens ** (-0.5)
    gathered = lax.all_gather(vectors, "dp", axis=0, tiled=True)
    total, feat = gathered.shape
    dp_index, tensor_index = lax.axis_index("dp"), lax.axis_index("tensor")
    row_width, col_width = feat // lax.axis_size("dp"), feat // lax.axis_size("tensor")
    cols = lax.dynamic_slice_in_dim(gathered, tensor_index * col_width, col_width, 1)
    rows = lax.dynamic_slice_in_dim(gathered, dp_index * row_width, row_width, 1)
    fisher = lax.dot_general(rows, cols, TN, precision=lax.Precision.HIGHEST) / total
    owners = dp_index * local + jnp.arange(local, dtype=jnp.int32)
    selector = (assignment[None, :] == owners[:, None]).astype(jnp.float32)
    return jnp.dot(selector, cols, precision=lax.Precision.HIGHEST), fisher


def on_device(*arrays):
    local = arrays[0].shape[1]
    if lax.axis_size("tensor") == 4 and lax.axis_size("dp") == 4 and local == 2:
        return two_level(*arrays)
    return any_sizes(*arrays)


def solution(mesh):
    return jax.shard_map(
        on_device,
        mesh=mesh,
        in_specs=(
            P(None, ("groups", "dp"), None, "tensor"),
            P(None, ("groups", "dp"), None, "tensor"),
            P(None, "tensor", None),
            P(None, "tensor", None),
            P(("groups", "dp")),
            P("groups"),
        ),
        out_specs=(P(("groups", "dp"), "tensor"), P(("groups", "dp"), "tensor")),
        check_vma=False,
    )
```
